256 devices in a mesh: rep: 16 (over x, y_lo, core), fsdp: 16 (over z, y_hi).
Axes of the slice: x: 4, y: 4 (y_hi: 2, y_lo: 2; y = y_hi * 2 + y_lo), z: 8, core: 2. Of those that a mesh axis runs over, the one named last changes fastest.
Arguments:
- grad_parts: bfloat16 [16, 16, 1024, 4096], P('rep', 'fsdp')
- momentum: float32 [16, 1024, 4096], P('rep', 'fsdp'), may hold values from -24 to 24
- band: int32 [32], replicated, may hold values from 0 to 4095, as said below
Outputs:
- new_momentum: float32 [16, 1024, 4096], P('rep', 'fsdp')
- step_dir: float32 [1024, 4096], P('fsdp')
The draws below stay inside these ranges and needn't reach their ends.
Inputs may be any that keep to these rules, and one draw needn't show every extreme that they name: `band`: 32 distinct indices; 0 and 4095 are always among them.
All inputs are finite; a program needn't handle non-finite values.
Results may differ from the reference program's by a relative error of at most 0.0003.
Values sent between devices are 32-bit elements; how exact they have to be, the bound alone decides.
No kernel may reach another device: no remote copies, remote signals or barrier semaphores. Data moves between devices by JAX's collectives and lax.ppermute only.
A program may use at most 128 MiB of HBM per device.

```python
import math
import jax
import jax.numpy as jnp
from jax import lax

SPAN = 64
BAND = 32
COLS = 4096
ROWS_DEV = 64
ROWS = 1024
N_REP = 16
N_FSDP = 16


def draw_grad_parts(key, part):
    key = jax.random.fold_in(key, 11)
    keys = jax.random.split(key, 3)
    shape = (N_REP, N_FSDP, ROWS, COLS)
    row_scale = jnp.exp(jax.random.uniform(keys[1], (ROWS,), jnp.float32, 0.0, math.log(10.0)))
    col_scale = jnp.exp(jax.random.uniform(keys[2], (COLS,), jnp.float32, 0.0, math.log(10.0)))
    block = (jnp.arange(ROWS) // ROWS_DEV).astype(jnp.float32)
    ramp = jnp.exp(math.log(3.0) * block / max(N_FSDP - 1, 1))
    noise = jax.random.normal(keys[0], shape, jnp.float32)
    scale = (row_scale * ramp)[:, None] * col_scale[None, :]
    return (0.1 * noise * scale[None, None]).astype(jnp.bfloat16)


def draw_band(key, part):
    key = jax.random.fold_in(key, 23)
    keys = jax.random.split(key, 2)
    total = SPAN * SPAN
    inner = jax.random.permutation(keys[0], total - 2)[:BAND - 2] + 1
    values = jnp.concatenate([jnp.zeros((1,), jnp.int32), inner.astype(jnp.int32), jnp.full((1,), total - 1, jnp.int32)])
    order = jax.random.permutation(keys[1], BAND)
    return values[order].astype(jnp.int32)


def shard_levels(stream_key, dims, pieces, smallest, largest):
    def one(axis_at, blocks):
        draws = jax.random.uniform(jax.random.fold_in(jax.random.fold_in(stream_key, 6), axis_at), (blocks,), jnp.float32, smallest / len(pieces), largest / len(pieces))
        return jnp.repeat(jnp.exp(draws), dims[axis_at] // blocks).reshape((-1,) + (1,) * (len(dims) - axis_at - 1))

    factor_of = one(*pieces[0])
    for cut in pieces[1:]:
        factor_of = factor_of * one(*cut)
    return factor_of


def centred(own_key, extent, scale, limit, pieces=(), kind=jnp.bfloat16):
    entries = jax.random.normal(own_key, extent, jnp.float32) * scale
    if len(pieces) > 0:
        entries = shard_levels(own_key, extent, pieces, -0.22, 0.18) * entries
    return jnp.clip(entries, min=-limit, max=limit).astype(kind)


def setup_inputs(seed: int = 0) -> dict:
    key_of = jax.random.split(jax.random.key(seed), 4)
    grad_parts = draw_grad_parts(jax.random.fold_in(key_of[3], 71), 0)
    momentum = centred(key_of[1], (N_REP, ROWS, COLS), 4.0, 24.0, ((0, 16), (1, 16)), jnp.float32)
    band = draw_band(jax.random.fold_in(key_of[3], 71), 0)
    return dict(grad_parts=grad_parts, momentum=momentum, band=band)


def dct_table(index):
    pos = jnp.arange(SPAN).astype(jnp.float32)
    freq = index.astype(jnp.float32)[:, None]
    table = jnp.cos(jnp.pi * (2.0 * pos[None, :] + 1.0) * freq / (2.0 * SPAN)) * jnp.sqrt(2.0 / SPAN)
    return jnp.where(index[:, None] == 0, jnp.sqrt(1.0 / SPAN) * jnp.ones_like(table), table)

def make_basis(band):
    first = dct_table(band // SPAN)
    second = dct_table(band % SPAN)
    return (first[:, :, None] * second[:, None, :]).reshape(BAND, SPAN * SPAN)

def project(field, basis):
    row_blocks = field.shape[0] // SPAN
    col_blocks = field.shape[1] // SPAN
    blocks = field.reshape(row_blocks, SPAN, col_blocks, SPAN).transpose(0, 2, 1, 3)
    blocks = blocks.reshape(row_blocks * col_blocks, SPAN * SPAN)
    coeffs = jnp.dot(blocks, basis.T, precision=lax.Precision.HIGHEST)
    return coeffs.reshape(row_blocks, col_blocks, BAND)

def decode(coeffs, basis):
    row_blocks, col_blocks = (coeffs.shape[0], coeffs.shape[1])
    flat = jnp.dot(coeffs.reshape(-1, BAND), basis, precision=lax.Precision.HIGHEST)
    flat = flat.reshape(row_blocks, col_blocks, SPAN, SPAN).transpose(0, 2, 1, 3)
    return flat.reshape(row_blocks * SPAN, col_blocks * SPAN)

def reference(grad_parts, momentum, band):
    basis = make_basis(band)

    def one_replica(pair):
        parts, previous = pair
        grad = lax.optimization_barrier(jnp.sum(parts.astype(jnp.float32), axis=0))
        mom = 0.9 * previous + grad
        coeffs = project(mom, basis)
        return (mom - decode(coeffs, basis), coeffs)
    new_momentum, coeffs = lax.map(one_replica, (grad_parts, momentum))
    mean_coeffs = lax.optimization_barrier(jnp.mean(coeffs, axis=0))
    average = decode(mean_coeffs, basis)
    step_dir = average * lax.rsqrt(jnp.mean(average * average) + 1e-06)
    return (new_momentum, step_dir)
```

```python
import functools

import jax
import jax.numpy as jnp
import numpy as np
from jax import lax
from jax.experimental import pallas as pl
from jax.experimental.pallas import tpu as pltpu
from jax.sharding import Mesh, PartitionSpec as P

SPAN = 64
BAND = 32
COLS = 4096
ROWS = 1024
NZ = 8
REPS = 16
HIGHEST = lax.Precision.HIGHEST
VMEM_LIMIT = 16 * 1024 * 1024
NO_COST = pl.CostEstimate(flops=0, bytes_accessed=0, transcendentals=0)

CHUNK, Y_COLS = 1536, 1024
Y_AT = 2 * CHUNK


def dct_table(index):
    pos = jnp.arange(SPAN).astype(jnp.float32)
    freq = index.astype(jnp.float32)[:, None]
    table = jnp.cos(jnp.pi * (2.0 * pos[None, :] + 1.0) * freq / (2.0 * SPAN)) * jnp.sqrt(
        2.0 / SPAN
    )
    return jnp.where(index[:, None] == 0, jnp.sqrt(1.0 / SPAN) * jnp.ones_like(table), table)


def thirds(x):
    high = x.astype(jnp.bfloat16)
    rest = x - high.astype(jnp.float32)
    middle = rest.astype(jnp.bfloat16)
    low = (rest - middle.astype(jnp.float32)).astype(jnp.bfloat16)
    return high, middle, low


def dot(a, b):
    return jnp.dot(a, b, preferred_element_type=jnp.float32)


def add_thirds(stacked):
    n = stacked.shape[0] // 3
    return (stacked[2 * n :] + stacked[n : 2 * n]) + stacked[:n]


def along_blocks(x, ones):
    return add_thirds(dot(jnp.concatenate(thirds(x), axis=0), ones))


def partial_coeffs_kernel(where_ref, grad_ref, mom_ref, first_ref, second_ref, ones_ref, out_ref):
    first3 = jnp.concatenate(thirds(first_ref[...]), axis=0)
    total = jnp.zeros((BAND, 128), jnp.float32)
    for half in range(2):
        rows = grad_ref[half * SPAN : (half + 1) * SPAN, :]
        along = add_thirds(dot(first3, rows)) * second_ref[...]
        total += along_blocks(along, ones_ref[half])
    out_ref[0] = total

    @pl.when(pl.program_id(0) == where_ref[0])
    def _():
        along = jnp.dot(
            first_ref[...], mom_ref[...], precision=HIGHEST, preferred_element_type=jnp.float32
        )
        along = (0.9 * along) * second_ref[...]
        out_ref[0] += along_blocks(along, ones_ref[where_ref[1]])


def partial_coeffs(where, grad, mom, first, second, ones):
    fixed = lambda shape: pl.BlockSpec(shape, lambda i, w: (0,) * len(shape))
    return pl.pallas_call(
        partial_coeffs_kernel,
        out_shape=jax.ShapeDtypeStruct((NZ, BAND, 128), jnp.float32),
        grid_spec=pltpu.PrefetchScalarGridSpec(
            num_scalar_prefetch=1,
            grid=(NZ,),
            in_specs=[
                pl.BlockSpec((2 * SPAN, COLS), lambda i, w: (i, 0)),
                fixed((SPAN, COLS)),
                fixed((BAND, SPAN)),
                fixed((BAND, COLS)),
                fixed((2, COLS, 128)),
            ],
            out_specs=pl.BlockSpec((1, BAND, 128), lambda i, w: (i, 0, 0)),
        ),
        compiler_params=pltpu.CompilerParams(vmem_limit_bytes=2 * VMEM_LIMIT),
        cost_estimate=NO_COST,
        name="partial_coeffs",
    )(where, grad, mom, first, second, ones)


def new_momentum(mom_ref, parts, first_ref, second_ref, same_ref):
    grad = parts[0][...]
    for part in parts[1:]:
        grad = grad + part[...]
    if grad.shape[0] == 2 * SPAN:
        grad = jnp.concatenate([grad[:SPAN], grad[SPAN:]], axis=1)
    mom = 0.9 * mom_ref[...] + grad
    first, second = first_ref[...], second_ref[...]
    along = jnp.dot(first, mom, precision=HIGHEST, preferred_element_type=jnp.float32)
    spread = [
        along_blocks(along[:, c : c + 128] * second, same_ref[...]) * second
        for c in range(0, mom.shape[1], 128)
    ]
    own = lax.dot_general(
        first, jnp.concatenate(spread, axis=1), (((0,), (0,)), ((), ())), precision=HIGHEST,
        preferred_element_type=jnp.float32,
    )
    return mom - own


def finish_kernel(mom_ref, *refs):
    *parts, first_ref, second_ref, same_ref, out_ref = refs
    out_ref[...] = new_momentum(mom_ref, parts, first_ref, second_ref, same_ref)


def whole(x):
    return pl.BlockSpec(x.shape, lambda i: (0, 0))


def finish(mom, at, width, parts, first, second, same):
    others = (*parts, first, second, same)
    return pl.pallas_call(
        finish_kernel,
        out_shape=jax.ShapeDtypeStruct((SPAN, width), jnp.float32),
        grid=(1,),
        in_specs=[pl.BlockSpec((SPAN, width), lambda i: (0, at // width)), *map(whole, others)],
        out_specs=pl.BlockSpec((SPAN, width), lambda i: (0, 0)),
        compiler_params=pltpu.CompilerParams(vmem_limit_bytes=VMEM_LIMIT),
        cost_estimate=NO_COST,
        name="finish",
    )(mom, *others)


def last_kernel(n_fronts, *refs):
    squares_ref, more_ref, average_ref = refs[n_fronts : n_fronts + 3]
    mom_ref, *parts, first_ref, second_ref, same_ref, out_ref, dir_ref = refs[n_fronts + 3 :]
    mean_square = jnp.sum(squares_ref[...] + more_ref[...]) / (ROWS * COLS) + 1e-06
    scale = lax.rsqrt(mean_square)
    scale = scale * (1.5 - 0.5 * (mean_square * scale) * scale)
    dir_ref[...] = average_ref[...] * scale
    at = 0
    for ref in refs[:n_fronts]:
        out_ref[:, at : at + ref.shape[1]] = ref[...]
        at += ref.shape[1]
    out_ref[:, at:] = new_momentum(mom_ref, parts, first_ref, second_ref, same_ref)


def last(fronts, squares, more, average, mom, at, width, parts, first, second, same):
    before, others = (*fronts, squares, more, average), (*parts, first, second, same)
    out = jax.ShapeDtypeStruct((SPAN, COLS), jnp.float32)
    return pl.pallas_call(
        functools.partial(last_kernel, len(fronts)),
        out_shape=[out, out],
        grid=(1,),
        in_specs=[
            *map(whole, before),
            pl.BlockSpec((SPAN, width), lambda i: (0, at // width)),
            *map(whole, others),
        ],
        out_specs=[whole(out), whole(out)],
        compiler_params=pltpu.CompilerParams(vmem_limit_bytes=VMEM_LIMIT),
        cost_estimate=NO_COST,
        name="last",
    )(*before, mom, *others)


def decode_kernel(where_ref, coeffs_ref, first_ref, second_ref, spread_ref, out_ref):
    along = along_blocks(coeffs_ref[...], spread_ref[where_ref[1]]) * second_ref[...]
    out_ref[...] = lax.dot_general(
        first_ref[...], along, (((0,), (0,)), ((), ())), precision=HIGHEST,
        preferred_element_type=jnp.float32,
    )


def decode(where, coeffs, first, second, spread):
    vmem = pl.BlockSpec(memory_space=pltpu.VMEM)
    return pl.pallas_call(
        decode_kernel,
        out_shape=jax.ShapeDtypeStruct((SPAN, COLS), jnp.float32),
        in_specs=[pl.BlockSpec(memory_space=pltpu.SMEM)] + [vmem] * 4,
        compiler_params=pltpu.CompilerParams(vmem_limit_bytes=VMEM_LIMIT),
        cost_estimate=NO_COST,
        name="decode",
    )(where, coeffs, first, second, spread)


def flip(x, axis, size, bit):
    return lax.ppermute(x, axis, [(i, i ^ bit) for i in range(size)])


def up(x):
    return lax.ppermute(x, "z", [(i, (i + 1) % NZ) for i in range(NZ)])


def down(x):
    return lax.ppermute(x, "z", [(i, (i - 1) % NZ) for i in range(NZ)])


def after(x, *earlier):
    return lax.optimization_barrier((x, *earlier))[0]


def add_four(terms):
    own, one, two, three = terms
    return (own + one) + (two + three)


def swap(x, axes, flips):
    sizes = [lax.axis_size(axis) for axis in axes]
    places = list(np.ndindex(*sizes))
    index = lambda place: int(np.ravel_multi_index(place, sizes))
    return lax.ppermute(x, axes, [(index(p), index([i ^ f for i, f in zip(p, flips)])) for p in places])


def swap_three(x, axes, one, two):
    return [x] + [swap(x, axes, flips) for flips in ((one, 0), (0, two), (one, two))]


def squares_kernel(coeffs_ref, gram_ref, out_ref):
    total = jnp.zeros((BAND, 128), jnp.float32)
    for i in range(coeffs_ref.shape[0]):
        coeffs = coeffs_ref[i]
        total += coeffs * jnp.dot(
            gram_ref[...], coeffs, precision=HIGHEST, preferred_element_type=jnp.float32
        )
    out_ref[...] = (total[:8] + total[8:16]) + (total[16:24] + total[24:])


def squares_of(coeffs, gram):
    return pl.pallas_call(
        squares_kernel,
        out_shape=jax.ShapeDtypeStruct((8, 128), jnp.float32),
        cost_estimate=NO_COST,
        name="squares",
    )(coeffs, gram)


class Ring:
    def __init__(self, block, width):
        self.block, self.width = block, width
        self.step = 4
        self.first = block(4)
        self.going = None

    def next(self):
        half = self.width // 2
        if self.step == 4:
            terms = self.first[:, :half], self.first[:, half:]
        else:
            upward, downward = self.going
            if self.step == 3:
                zeros = jnp.zeros((upward.shape[0], half), jnp.float32)
                upward = jnp.concatenate([upward, zeros], axis=1)
                downward = jnp.concatenate([zeros, downward], axis=1)
            terms = self.block(self.step) + upward, self.block(-self.step) + downward
        self.step -= 1
        return terms

    def parts(self):
        return [self.block(0), *self.going]


class Flight:
    def __init__(self, *rings):
        self.rings = rings
        terms = [ring.next() for ring in rings]
        self.widths = [up_term.shape[1] for up_term, _ in terms]
        self.sent = [jnp.concatenate(list(side), axis=1) if len(terms) > 1 else side[0] for side in zip(*terms)]
        self.got = [up(self.sent[0]), down(self.sent[1])]

    def land(self, got):
        at = 0
        for ring, width in zip(self.rings, self.widths):
            ring.going = [side[:, at : at + width] for side in got]
            at += width


def meet(*arrays):
    return lax.optimization_barrier(arrays)


def per_device(grad_parts, momentum, band):
    z, yh = lax.axis_index("z"), lax.axis_index("yh")
    where = jnp.stack([z, yh]).astype(jnp.int32)
    grad = grad_parts[0, 0]
    mom = momentum[0]

    first = dct_table(band // SPAN)
    second_table = dct_table(band % SPAN)
    second = jnp.tile(second_table, (1, COLS // SPAN))
    block_of = np.arange(COLS) // SPAN
    ones = np.zeros((2, COLS, 128), np.float32)
    for half in range(2):
        ones[half, np.arange(COLS), half * 64 + block_of] = 1.0
    spread = jnp.asarray(ones.transpose(0, 2, 1), jnp.bfloat16)
    ones = jnp.asarray(ones, jnp.bfloat16)
    same = jnp.asarray(np.kron(np.eye(2), np.ones((SPAN, SPAN))), jnp.bfloat16)

    def owner(k):
        return lax.rem(z + k + NZ, NZ)

    def z_block(at):
        def block(k):
            rows = lax.dynamic_slice(grad, (owner(k) * 2 * SPAN, at), (2 * SPAN, CHUNK))
            return rows.astype(jnp.float32)

        return block

    def y_block(got):
        def block(k):
            rows = lax.dynamic_slice(grad, ((owner(k) * 2 + yh) * SPAN, Y_AT), (SPAN, Y_COLS))
            term = lax.dynamic_index_in_dim(got, owner(k), 0, keepdims=False) + rows.astype(jnp.float32)
            return jnp.concatenate([term[:, : Y_COLS // 2], term[:, Y_COLS // 2 :]], axis=0)

        return block

    def cross_y(total):
        give = lax.dynamic_slice(total, ((1 - yh) * SPAN, 0), (SPAN, CHUNK))
        keep = lax.dynamic_slice(total, (yh * SPAN, 0), (SPAN, CHUNK))
        return keep, give, flip(give, "yh", 2, 1)

    ring_a, ring_b = Ring(z_block(0), CHUNK), Ring(z_block(CHUNK), CHUNK)
    a = Flight(ring_a)
    ring_b.first = meet(ring_b.first, *a.sent)[0]
    b = Flight(ring_b)
    rows = after(grad, *b.sent).reshape(NZ, 2 * SPAN, COLS)
    give = lax.dynamic_slice(rows, (0, (1 - yh) * SPAN, Y_AT), (NZ, SPAN, Y_COLS)).astype(jnp.float32)
    got = flip(give, "yh", 2, 1)

    a.land(meet(*a.got, give)[:2])
    a = Flight(ring_a)

    b.land(meet(*b.got, *a.sent)[:2])
    b = Flight(ring_b)
    coeffs = partial_coeffs(where, grad, after(mom, *b.sent), first, second, ones)
    pair = second[:, :128]
    gram = jnp.dot(first, first.T, precision=HIGHEST) * jnp.dot(second_table, second_table.T, precision=HIGHEST)

    coeffs, pair, *rest = meet(coeffs, pair, *a.got)
    a.land(rest)
    a = Flight(ring_a)

    got, coeffs, *rest = meet(got, coeffs, *b.got, *a.sent)
    b.land(rest[:2])
    ring_y = Ring(y_block(got), Y_COLS // 2)
    b = Flight(ring_b, ring_y)
    coeffs = coeffs + flip(coeffs, "c", 2, 1)
    coeffs = coeffs + flip(coeffs, "x", 4, 1)

    coeffs, *rest = meet(coeffs, *a.got, *b.sent)
    a.land(rest[:2])
    a = Flight(ring_a)
    coeffs = coeffs + flip(coeffs, "x", 4, 2)
    coeffs = coeffs + flip(coeffs, "yl", 2, 1)
    coeffs = coeffs + flip(coeffs, "yh", 2, 1)

    coeffs, *rest = meet(coeffs, *b.got, *a.sent)
    b.land(rest[:2])
    b = Flight(ring_b, ring_y)
    pairs = coeffs.reshape(4, 2, BAND, 128)
    side = z % 2
    keep = lax.dynamic_index_in_dim(pairs, side, 1, keepdims=False)
    other = lax.dynamic_index_in_dim(pairs, 1 - side, 1, keepdims=False)
    more = flip(other, "z", NZ, 1)

    a.land(meet(*a.got, *b.sent, other)[:2])
    keep_a, give_a, got_a = cross_y(sum(ring_a.parts()))

    front_a = finish(mom, 0, CHUNK, [keep_a, got_a], first, pair, same)

    front_a, keep, more, *rest = meet(front_a, keep, more, *b.got)
    b.land(rest)
    y = Flight(ring_y)
    keep_b, give_b, got_b = cross_y(after(sum(ring_b.parts()), *y.sent))
    coeffs = after(keep, give_b) + more
    coeffs = coeffs + flip(coeffs, "z", NZ, 2)

    coeffs, *rest = meet(coeffs, *y.got)
    y.land(rest)
    y = Flight(ring_y)
    coeffs = after(coeffs, *y.sent)
    coeffs = (coeffs + flip(coeffs, "z", NZ, 4)) * (1.0 / REPS)

    squares = squares_of(coeffs, gram)
    more = flip(squares, "z", NZ, 1)
    coeffs = lax.dynamic_index_in_dim(coeffs, z // 2, 0, keepdims=False)
    average = decode(where, after(coeffs, squares), first, second, spread)
    front_b = finish(mom, CHUNK, CHUNK, [keep_b, after(got_b, average)], first, pair, same)

    front_b, average, squares, more, *rest = meet(front_b, average, squares, more, *y.got)
    y.land(rest)
    momentum, step_dir = last(
        [front_a, front_b], squares, more, average, mom, Y_AT, Y_COLS, ring_y.parts(), first, pair, same
    )
    return (momentum[None], step_dir)


def solution(mesh):
    fine = Mesh(mesh.devices.reshape(4, 2, 2, NZ, 2), ("x", "yl", "c", "z", "yh"))
    rep, fsdp = ("x", "yl", "c"), ("z", "yh")
    return jax.shard_map(
        per_device,
        mesh=fine,
        in_specs=(P(rep, fsdp, None, None), P(rep, fsdp, None), P()),
        out_specs=(P(rep, fsdp, None), P(fsdp, None)),
        check_vma=False,
    )
```

```python
import functools

import jax
import jax.numpy as jnp
import numpy as np
from jax import lax
from jax.experimental import pallas as pl
from jax.experimental.pallas import tpu as pltpu
from jax.sharding import Mesh, PartitionSpec as P

SPAN = 64
BAND = 32
COLS = 4096
ROWS = 1024
NZ = 8
REPS = 16
HIGHEST = lax.Precision.HIGHEST
VMEM_LIMIT = 16 * 1024 * 1024
NO_COST = pl.CostEstimate(flops=0, bytes_accessed=0, transcendentals=0)

CHUNK, Y_COLS = 1536, 1024
Y_AT = 2 * CHUNK


def dct_table(index):
    pos = jnp.arange(SPAN).astype(jnp.float32)
    freq = index.astype(jnp.float32)[:, None]
    table = jnp.cos(jnp.pi * (2.0 * pos[None, :] + 1.0) * freq / (2.0 * SPAN)) * jnp.sqrt(
        2.0 / SPAN
    )
    return jnp.where(index[:, None] == 0, jnp.sqrt(1.0 / SPAN) * jnp.ones_like(table), table)


def thirds(x):
    high = x.astype(jnp.bfloat16)
    rest = x - high.astype(jnp.float32)
    middle = rest.astype(jnp.bfloat16)
    low = (rest - middle.astype(jnp.float32)).astype(jnp.bfloat16)
    return high, middle, low


def dot(a, b):
    return jnp.dot(a, b, preferred_element_type=jnp.float32)


def add_thirds(stacked):
    n = stacked.shape[0] // 3
    return (stacked[2 * n :] + stacked[n : 2 * n]) + stacked[:n]


def along_blocks(x, ones):
    return add_thirds(dot(jnp.concatenate(thirds(x), axis=0), ones))


def partial_coeffs_kernel(where_ref, grad_ref, mom_ref, first_ref, second_ref, ones_ref, out_ref):
    first3 = jnp.concatenate(thirds(first_ref[...]), axis=0)
    total = jnp.zeros((BAND, 128), jnp.float32)
    for half in range(2):
        rows = grad_ref[half * SPAN : (half + 1) * SPAN, :]
        along = add_thirds(dot(first3, rows)) * second_ref[...]
        total += along_blocks(along, ones_ref[half])
    out_ref[0] = total

    @pl.when(pl.program_id(0) == where_ref[0])
    def _():
        along = jnp.dot(
            first_ref[...], mom_ref[...], precision=HIGHEST, preferred_element_type=jnp.float32
        )
        along = (0.9 * along) * second_ref[...]
        out_ref[0] += along_blocks(along, ones_ref[where_ref[1]])


def partial_coeffs(where, grad, mom, first, second, ones):
    fixed = lambda shape: pl.BlockSpec(shape, lambda i, w: (0,) * len(shape))
    return pl.pallas_call(
        partial_coeffs_kernel,
        out_shape=jax.ShapeDtypeStruct((NZ, BAND, 128), jnp.float32),
        grid_spec=pltpu.PrefetchScalarGridSpec(
            num_scalar_prefetch=1,
            grid=(NZ,),
            in_specs=[
                pl.BlockSpec((2 * SPAN, COLS), lambda i, w: (i, 0)),
                fixed((SPAN, COLS)),
                fixed((BAND, SPAN)),
                fixed((BAND, COLS)),
                fixed((2, COLS, 128)),
            ],
            out_specs=pl.BlockSpec((1, BAND, 128), lambda i, w: (i, 0, 0)),
        ),
        compiler_params=pltpu.CompilerParams(vmem_limit_bytes=2 * VMEM_LIMIT),
        cost_estimate=NO_COST,
        name="partial_coeffs",
    )(where, grad, mom, first, second, ones)


def new_momentum(mom_ref, parts, first_ref, second_ref, same_ref):
    grad = parts[0][...]
    for part in parts[1:]:
        grad = grad + part[...]
    if grad.shape[0] == 2 * SPAN:
        grad = jnp.concatenate([grad[:SPAN], grad[SPAN:]], axis=1)
    mom = 0.9 * mom_ref[...] + grad
    first, second = first_ref[...], second_ref[...]
    along = jnp.dot(first, mom, precision=HIGHEST, preferred_element_type=jnp.float32)
    spread = [
        along_blocks(along[:, c : c + 128] * second, same_ref[...]) * second
        for c in range(0, mom.shape[1], 128)
    ]
    own = lax.dot_general(
        first, jnp.concatenate(spread, axis=1), (((0,), (0,)), ((), ())), precision=HIGHEST,
        preferred_element_type=jnp.float32,
    )
    return mom - own


def finish_kernel(has_front, mom_ref, *refs):
    *parts, first_ref, second_ref, same_ref, out_ref = refs[has_front:]
    out_ref[...] = new_momentum(mom_ref, parts, first_ref, second_ref, same_ref)


def whole(x):
    return pl.BlockSpec(x.shape, lambda i: (0, 0))


def finish(front, mom, at, width, parts, first, second, same):
    front = [] if front is None else [front]
    others = (*parts, first, second, same)
    columns = pl.BlockSpec((SPAN, width), lambda i: (0, at // width))
    return pl.pallas_call(
        functools.partial(finish_kernel, len(front)),
        out_shape=jax.ShapeDtypeStruct((SPAN, COLS), jnp.float32),
        grid=(1,),
        in_specs=[columns, *[pl.BlockSpec(memory_space=pl.ANY)] * len(front), *map(whole, others)],
        out_specs=columns,
        input_output_aliases={1: 0} if front else {},
        compiler_params=pltpu.CompilerParams(vmem_limit_bytes=VMEM_LIMIT),
        cost_estimate=NO_COST,
        name="finish",
    )(mom, *front, *others)


def last_kernel(front_ref, squares_ref, more_ref, average_ref, mom_ref, *refs):
    *parts, first_ref, second_ref, same_ref, out_ref, dir_ref = refs
    mean_square = jnp.sum(squares_ref[...] + more_ref[...]) / (ROWS * COLS) + 1e-06
    scale = lax.rsqrt(mean_square)
    scale = scale * (1.5 - 0.5 * (mean_square * scale) * scale)
    dir_ref[...] = average_ref[...] * scale
    out_ref[...] = new_momentum(mom_ref, parts, first_ref, second_ref, same_ref)


def last(front, squares, more, average, mom, at, width, parts, first, second, same):
    before, others = (squares, more, average), (*parts, first, second, same)
    out = jax.ShapeDtypeStruct((SPAN, COLS), jnp.float32)
    columns = pl.BlockSpec((SPAN, width), lambda i: (0, at // width))
    return pl.pallas_call(
        last_kernel,
        out_shape=[out, out],
        grid=(1,),
        in_specs=[pl.BlockSpec(memory_space=pl.ANY), *map(whole, before), columns, *map(whole, others)],
        out_specs=[columns, whole(out)],
        input_output_aliases={0: 0},
        compiler_params=pltpu.CompilerParams(vmem_limit_bytes=VMEM_LIMIT),
        cost_estimate=NO_COST,
        name="last",
    )(front, *before, mom, *others)


def average_kernel(where_ref, coeffs_ref, more_ref, gram_ref, first_ref, second_ref, spread_ref, squares_ref, out_ref):
    total = jnp.zeros((BAND, 128), jnp.float32)
    for i in range(coeffs_ref.shape[0]):
        coeffs = (coeffs_ref[i] + more_ref[i]) * (1.0 / REPS)
        total += coeffs * jnp.dot(
            gram_ref[...], coeffs, precision=HIGHEST, preferred_element_type=jnp.float32
        )
    squares_ref[...] = (total[:8] + total[8:16]) + (total[16:24] + total[24:])
    row = where_ref[0] // 2
    coeffs = (coeffs_ref[row] + more_ref[row]) * (1.0 / REPS)
    half = COLS // SPAN
    coeffs = jnp.where(where_ref[1] == 0, coeffs[:, :half], coeffs[:, half:])
    along = along_blocks(coeffs, spread_ref[...]) * second_ref[...]
    out_ref[...] = lax.dot_general(
        first_ref[...], along, (((0,), (0,)), ((), ())), precision=HIGHEST,
        preferred_element_type=jnp.float32,
    )


def average_of(where, coeffs, more, gram, first, second, spread):
    vmem = pl.BlockSpec(memory_space=pltpu.VMEM)
    return pl.pallas_call(
        average_kernel,
        out_shape=[jax.ShapeDtypeStruct((8, 128), jnp.float32), jax.ShapeDtypeStruct((SPAN, COLS), jnp.float32)],
        in_specs=[pl.BlockSpec(memory_space=pltpu.SMEM)] + [vmem] * 6,
        compiler_params=pltpu.CompilerParams(vmem_limit_bytes=VMEM_LIMIT),
        cost_estimate=NO_COST,
        name="average",
    )(where, coeffs, more, gram, first, second, spread)


def flip(x, axis, size, bit):
    return lax.ppermute(x, axis, [(i, i ^ bit) for i in range(size)])


def up(x):
    return lax.ppermute(x, "z", [(i, (i + 1) % NZ) for i in range(NZ)])


def down(x):
    return lax.ppermute(x, "z", [(i, (i - 1) % NZ) for i in range(NZ)])


def after(x, *earlier):
    return lax.optimization_barrier((x, *earlier))[0]


def add_four(terms):
    own, one, two, three = terms
    return (own + one) + (two + three)


def swap(x, axes, flips):
    sizes = [lax.axis_size(axis) for axis in axes]
    places = list(np.ndindex(*sizes))
    index = lambda place: int(np.ravel_multi_index(place, sizes))
    return lax.ppermute(x, axes, [(index(p), index([i ^ f for i, f in zip(p, flips)])) for p in places])


def swap_three(x, axes, one, two):
    return [x] + [swap(x, axes, flips) for flips in ((one, 0), (0, two), (one, two))]


class Ring:
    def __init__(self, block, width):
        self.block, self.width = block, width
        self.step = 4
        self.first = block(4)
        self.going = None

    def next(self):
        half = self.width // 2
        if self.step == 4:
            terms = self.first[:, :half], self.first[:, half:]
        else:
            upward, downward = self.going
            if self.step == 3:
                zeros = jnp.zeros((upward.shape[0], half), jnp.float32)
                upward = jnp.concatenate([upward, zeros], axis=1)
                downward = jnp.concatenate([zeros, downward], axis=1)
            terms = self.block(self.step) + upward, self.block(-self.step) + downward
        self.step -= 1
        return terms

    def parts(self):
        return [self.block(0), *self.going]


class Flight:
    def __init__(self, *rings):
        self.rings = rings
        terms = [ring.next() for ring in rings]
        self.widths = [up_term.shape[1] for up_term, _ in terms]
        self.sent = [jnp.concatenate(list(side), axis=1) if len(terms) > 1 else side[0] for side in zip(*terms)]
        self.got = [up(self.sent[0]), down(self.sent[1])]

    def land(self, got):
        at = 0
        for ring, width in zip(self.rings, self.widths):
            ring.going = [side[:, at : at + width] for side in got]
            at += width


def meet(*arrays):
    return lax.optimization_barrier(arrays)


def per_device(grad_parts, momentum, band):
    z, yh = lax.axis_index("z"), lax.axis_index("yh")
    where = jnp.stack([z, yh]).astype(jnp.int32)
    grad = grad_parts[0, 0]
    mom = momentum[0]

    first = dct_table(band // SPAN)
    second_table = dct_table(band % SPAN)
    second = jnp.tile(second_table, (1, COLS // SPAN))
    block_of = np.arange(COLS) // SPAN
    ones = np.zeros((2, COLS, 128), np.float32)
    for half in range(2):
        ones[half, np.arange(COLS), half * 64 + block_of] = 1.0
    spread = jnp.asarray(ones[0, :, : COLS // SPAN].T, jnp.bfloat16)
    ones = jnp.asarray(ones, jnp.bfloat16)
    same = jnp.asarray(np.kron(np.eye(2), np.ones((SPAN, SPAN))), jnp.bfloat16)

    def owner(k):
        return lax.rem(z + k + NZ, NZ)

    def z_block(at):
        def block(k):
            rows = lax.dynamic_slice(grad, (owner(k) * 2 * SPAN, at), (2 * SPAN, CHUNK))
            return rows.astype(jnp.float32)

        return block

    def y_block(got):
        def block(k):
            rows = lax.dynamic_slice(grad, ((owner(k) * 2 + yh) * SPAN, Y_AT), (SPAN, Y_COLS))
            term = lax.dynamic_index_in_dim(got, owner(k), 0, keepdims=False) + rows.astype(jnp.float32)
            return jnp.concatenate([term[:, : Y_COLS // 2], term[:, Y_COLS // 2 :]], axis=0)

        return block

    def cross_y(total):
        give = lax.dynamic_slice(total, ((1 - yh) * SPAN, 0), (SPAN, CHUNK))
        keep = lax.dynamic_slice(total, (yh * SPAN, 0), (SPAN, CHUNK))
        return keep, give, flip(give, "yh", 2, 1)

    ring_a, ring_b = Ring(z_block(0), CHUNK), Ring(z_block(CHUNK), CHUNK)
    a = Flight(ring_a)
    ring_b.first = meet(ring_b.first, *a.sent)[0]
    b = Flight(ring_b)
    rows = after(grad, *b.sent).reshape(NZ, 2 * SPAN, COLS)
    give = lax.dynamic_slice(rows, (0, (1 - yh) * SPAN, Y_AT), (NZ, SPAN, Y_COLS)).astype(jnp.float32)
    got = flip(give, "yh", 2, 1)

    a.land(meet(*a.got, give)[:2])
    a = Flight(ring_a)

    b.land(meet(*b.got, *a.sent)[:2])
    b = Flight(ring_b)
    coeffs = partial_coeffs(where, grad, after(mom, *b.sent), first, second, ones)
    pair = second[:, :128]
    gram = jnp.dot(first, first.T, precision=HIGHEST) * jnp.dot(second_table, second_table.T, precision=HIGHEST)

    coeffs, pair, *rest = meet(coeffs, pair, *a.got)
    a.land(rest)
    a = Flight(ring_a)

    got, coeffs, *rest = meet(got, coeffs, *b.got, *a.sent)
    b.land(rest[:2])
    ring_y = Ring(y_block(got), Y_COLS // 2)
    b = Flight(ring_b, ring_y)
    for axis, size, bit in (("c", 2, 1), ("x", 4, 1)):
        coeffs = coeffs + flip(coeffs, axis, size, bit)

    coeffs, *rest = meet(coeffs, *a.got, *b.sent)
    a.land(rest[:2])
    a = Flight(ring_a)
    coeffs = coeffs + flip(coeffs, "x", 4, 2)
    pairs = coeffs.reshape(4, 2, BAND, 128)
    keep = lax.dynamic_index_in_dim(pairs, z % 2, 1, keepdims=False)
    other = lax.dynamic_index_in_dim(pairs, 1 - z % 2, 1, keepdims=False)
    more = flip(other, "z", NZ, 1)

    keep, more, *rest = meet(keep, more, *b.got, *a.sent)
    b.land(rest[:2])
    b = Flight(ring_b, ring_y)
    coeffs = after(keep, *b.sent) + more
    coeffs = coeffs + flip(coeffs, "yl", 2, 1)

    coeffs, *rest = meet(coeffs, *a.got)
    a.land(rest)
    total = sum(ring_a.parts())
    keep_a = lax.dynamic_slice(total, (yh * SPAN, 0), (SPAN, CHUNK))
    give_a = lax.dynamic_slice(total, ((1 - yh) * SPAN, 0), (SPAN, CHUNK))
    flat = coeffs.reshape(2, SPAN, 128)
    got_a = flip(jnp.concatenate([give_a, flat[0], flat[1]], axis=1), "yh", 2, 1)
    got_a, more = got_a[:, :CHUNK], got_a[:, CHUNK:]
    coeffs = coeffs + jnp.stack([more[:, :128], more[:, 128:]]).reshape(4, BAND, 128)
    more = flip(coeffs, "z", NZ, 2)
    front = finish(None, mom, 0, CHUNK, [keep_a, after(got_a, coeffs)], first, pair, same)

    coeffs, more, front, *rest = meet(coeffs, more, front, *b.got)
    b.land(rest)
    y = Flight(ring_y)
    coeffs = after(coeffs, *y.sent) + more
    more = flip(coeffs, "z", NZ, 4)
    keep_b, give_b, got_b = cross_y(after(sum(ring_b.parts()), coeffs))

    y.land(meet(*y.got, give_b)[:2])
    y = Flight(ring_y)

    squares, average = average_of(where, after(coeffs, *y.sent), more, gram, first, second, spread)
    more = flip(squares, "z", NZ, 1)
    front = finish(front, mom, CHUNK, CHUNK, [keep_b, after(got_b, average)], first, pair, same)

    front, average, squares, more, *rest = meet(front, average, squares, more, *y.got)
    y.land(rest)
    momentum, step_dir = last(
        front, squares, more, average, mom, Y_AT, Y_COLS, ring_y.parts(), first, pair, same
    )
    return (momentum[None], step_dir)


def solution(mesh):
    fine = Mesh(mesh.devices.reshape(4, 2, 2, NZ, 2), ("x", "yl", "c", "z", "yh"))
    rep, fsdp = ("x", "yl", "c"), ("z", "yh")
    return jax.shard_map(
        per_device,
        mesh=fine,
        in_specs=(P(rep, fsdp, None, None), P(rep, fsdp, None), P()),
        out_specs=(P(rep, fsdp, None), P(fsdp, None)),
        check_vma=False,
    )
```

```python
import functools

import jax
import jax.numpy as jnp
import numpy as np
from jax import lax
from jax.experimental import pallas as pl
from jax.experimental.pallas import tpu as pltpu
from jax.sharding import Mesh, PartitionSpec as P

SPAN = 64
BAND = 32
COLS = 4096
ROWS = 1024
NZ = 8
REPS = 16
HIGHEST = lax.Precision.HIGHEST
VMEM_LIMIT = 16 * 1024 * 1024
NO_COST = pl.CostEstimate(flops=0, bytes_accessed=0, transcendentals=0)

CHUNK, Y_COLS = 1536, 1024
Y_AT = 2 * CHUNK


def dct_table(index):
    pos = jnp.arange(SPAN).astype(jnp.float32)
    freq = index.astype(jnp.float32)[:, None]
    table = jnp.cos(jnp.pi * (2.0 * pos[None, :] + 1.0) * freq / (2.0 * SPAN)) * jnp.sqrt(
        2.0 / SPAN
    )
    return jnp.where(index[:, None] == 0, jnp.sqrt(1.0 / SPAN) * jnp.ones_like(table), table)


def thirds(x):
    high = x.astype(jnp.bfloat16)
    rest = x - high.astype(jnp.float32)
    middle = rest.astype(jnp.bfloat16)
    low = (rest - middle.astype(jnp.float32)).astype(jnp.bfloat16)
    return high, middle, low


def dot(a, b):
    return jnp.dot(a, b, preferred_element_type=jnp.float32)


def add_thirds(stacked):
    n = stacked.shape[0] // 3
    return (stacked[2 * n :] + stacked[n : 2 * n]) + stacked[:n]


def along_blocks(x, ones):
    return add_thirds(dot(jnp.concatenate(thirds(x), axis=0), ones))


def partial_coeffs_kernel(where_ref, grad_ref, mom_ref, first_ref, second_ref, ones_ref, out_ref):
    first3 = jnp.concatenate(thirds(first_ref[...]), axis=0)
    total = jnp.zeros((BAND, 128), jnp.float32)
    for half in range(2):
        rows = grad_ref[half * SPAN : (half + 1) * SPAN, :]
        along = add_thirds(dot(first3, rows)) * second_ref[...]
        total += along_blocks(along, ones_ref[half])
    out_ref[0] = total

    @pl.when(pl.program_id(0) == where_ref[0])
    def _():
        along = jnp.dot(
            first_ref[...], mom_ref[...], precision=HIGHEST, preferred_element_type=jnp.float32
        )
        along = (0.9 * along) * second_ref[...]
        out_ref[0] += along_blocks(along, ones_ref[where_ref[1]])


def partial_coeffs(where, grad, mom, first, second, ones):
    fixed = lambda shape: pl.BlockSpec(shape, lambda i, w: (0,) * len(shape))
    return pl.pallas_call(
        partial_coeffs_kernel,
        out_shape=jax.ShapeDtypeStruct((NZ, BAND, 128), jnp.float32),
        grid_spec=pltpu.PrefetchScalarGridSpec(
            num_scalar_prefetch=1,
            grid=(NZ,),
            in_specs=[
                pl.BlockSpec((2 * SPAN, COLS), lambda i, w: (i, 0)),
                fixed((SPAN, COLS)),
                fixed((BAND, SPAN)),
                fixed((BAND, COLS)),
                fixed((2, COLS, 128)),
            ],
            out_specs=pl.BlockSpec((1, BAND, 128), lambda i, w: (i, 0, 0)),
        ),
        compiler_params=pltpu.CompilerParams(vmem_limit_bytes=2 * VMEM_LIMIT),
        cost_estimate=NO_COST,
        name="partial_coeffs",
    )(where, grad, mom, first, second, ones)


def new_momentum(mom_ref, parts, first_ref, second_ref, same_ref):
    grad = parts[0][...]
    for part in parts[1:]:
        grad = grad + part[...]
    if grad.shape[0] == 2 * SPAN:
        grad = jnp.concatenate([grad[:SPAN], grad[SPAN:]], axis=1)
    mom = 0.9 * mom_ref[...] + grad
    first, second = first_ref[...], second_ref[...]
    along = jnp.dot(first, mom, precision=HIGHEST, preferred_element_type=jnp.float32)
    spread = [
        along_blocks(along[:, c : c + 128] * second, same_ref[...]) * second
        for c in range(0, mom.shape[1], 128)
    ]
    own = lax.dot_general(
        first, jnp.concatenate(spread, axis=1), (((0,), (0,)), ((), ())), precision=HIGHEST,
        preferred_element_type=jnp.float32,
    )
    return mom - own


def finish_kernel(has_front, mom_ref, *refs):
    *parts, first_ref, second_ref, same_ref, out_ref = refs[has_front:]
    out_ref[...] = new_momentum(mom_ref, parts, first_ref, second_ref, same_ref)


def whole(x):
    return pl.BlockSpec(x.shape, lambda i: (0, 0))


def finish(front, mom, at, width, parts, first, second, same):
    front = [] if front is None else [front]
    others = (*parts, first, second, same)
    columns = pl.BlockSpec((SPAN, width), lambda i: (0, at // width))
    return pl.pallas_call(
        functools.partial(finish_kernel, len(front)),
        out_shape=jax.ShapeDtypeStruct((SPAN, COLS), jnp.float32),
        grid=(1,),
        in_specs=[columns, *[pl.BlockSpec(memory_space=pl.ANY)] * len(front), *map(whole, others)],
        out_specs=columns,
        input_output_aliases={1: 0} if front else {},
        compiler_params=pltpu.CompilerParams(vmem_limit_bytes=VMEM_LIMIT),
        cost_estimate=NO_COST,
        name="finish",
    )(mom, *front, *others)


def last_kernel(front_ref, squares_ref, more_ref, average_ref, mom_ref, *refs):
    *parts, first_ref, second_ref, same_ref, out_ref, dir_ref = refs
    mean_square = jnp.sum(squares_ref[...] + more_ref[...]) / (ROWS * COLS) + 1e-06
    scale = lax.rsqrt(mean_square)
    scale = scale * (1.5 - 0.5 * (mean_square * scale) * scale)
    dir_ref[...] = average_ref[...] * scale
    out_ref[...] = new_momentum(mom_ref, parts, first_ref, second_ref, same_ref)


def last(front, squares, more, average, mom, at, width, parts, first, second, same):
    before, others = (squares, more, average), (*parts, first, second, same)
    out = jax.ShapeDtypeStruct((SPAN, COLS), jnp.float32)
    columns = pl.BlockSpec((SPAN, width), lambda i: (0, at // width))
    return pl.pallas_call(
        last_kernel,
        out_shape=[out, out],
        grid=(1,),
        in_specs=[pl.BlockSpec(memory_space=pl.ANY), *map(whole, before), columns, *map(whole, others)],
        out_specs=[columns, whole(out)],
        input_output_aliases={0: 0},
        compiler_params=pltpu.CompilerParams(vmem_limit_bytes=VMEM_LIMIT),
        cost_estimate=NO_COST,
        name="last",
    )(front, *before, mom, *others)


def average_kernel(where_ref, coeffs_ref, more_ref, gram_ref, first_ref, second_ref, spread_ref, squares_ref, out_ref):
    total = jnp.zeros((BAND, 128), jnp.float32)
    for i in range(coeffs_ref.shape[0]):
        coeffs = (coeffs_ref[i] + more_ref[i]) * (1.0 / REPS)
        total += coeffs * jnp.dot(
            gram_ref[...], coeffs, precision=HIGHEST, preferred_element_type=jnp.float32
        )
    squares_ref[...] = (total[:8] + total[8:16]) + (total[16:24] + total[24:])
    row = lax.div(where_ref[0], 4) * 2 + lax.rem(where_ref[0], 2)
    coeffs = (coeffs_ref[row] + more_ref[row]) * (1.0 / REPS)
    half = COLS // SPAN
    coeffs = jnp.where(where_ref[1] == 0, coeffs[:, :half], coeffs[:, half:])
    along = along_blocks(coeffs, spread_ref[...]) * second_ref[...]
    out_ref[...] = lax.dot_general(
        first_ref[...], along, (((0,), (0,)), ((), ())), precision=HIGHEST,
        preferred_element_type=jnp.float32,
    )


def average_of(where, coeffs, more, gram, first, second, spread):
    vmem = pl.BlockSpec(memory_space=pltpu.VMEM)
    return pl.pallas_call(
        average_kernel,
        out_shape=[jax.ShapeDtypeStruct((8, 128), jnp.float32), jax.ShapeDtypeStruct((SPAN, COLS), jnp.float32)],
        in_specs=[pl.BlockSpec(memory_space=pltpu.SMEM)] + [vmem] * 6,
        compiler_params=pltpu.CompilerParams(vmem_limit_bytes=VMEM_LIMIT),
        cost_estimate=NO_COST,
        name="average",
    )(where, coeffs, more, gram, first, second, spread)


def flip(x, axis, size, bit):
    return lax.ppermute(x, axis, [(i, i ^ bit) for i in range(size)])


def up(x):
    return lax.ppermute(x, "z", [(i, (i + 1) % NZ) for i in range(NZ)])


def down(x):
    return lax.ppermute(x, "z", [(i, (i - 1) % NZ) for i in range(NZ)])


def after(x, *earlier):
    return lax.optimization_barrier((x, *earlier))[0]


def add_four(terms):
    own, one, two, three = terms
    return (own + one) + (two + three)


def swap(x, axes, flips):
    sizes = [lax.axis_size(axis) for axis in axes]
    places = list(np.ndindex(*sizes))
    index = lambda place: int(np.ravel_multi_index(place, sizes))
    return lax.ppermute(x, axes, [(index(p), index([i ^ f for i, f in zip(p, flips)])) for p in places])


def swap_three(x, axes, one, two):
    return [x] + [swap(x, axes, flips) for flips in ((one, 0), (0, two), (one, two))]


class Ring:
    def __init__(self, block, width):
        self.block, self.width = block, width
        self.step = 4
        self.first = block(4)
        self.going = None

    def next(self):
        half = self.width // 2
        if self.step == 4:
            terms = self.first[:, :half], self.first[:, half:]
        else:
            upward, downward = self.going
            if self.step == 3:
                zeros = jnp.zeros((upward.shape[0], half), jnp.float32)
                upward = jnp.concatenate([upward, zeros], axis=1)
                downward = jnp.concatenate([zeros, downward], axis=1)
            terms = self.block(self.step) + upward, self.block(-self.step) + downward
        self.step -= 1
        return terms

    def parts(self):
        return [self.block(0), *self.going]


class Flight:
    def __init__(self, *rings):
        self.rings = rings
        terms = [ring.next() for ring in rings]
        self.widths = [up_term.shape[1] for up_term, _ in terms]
        self.sent = [jnp.concatenate(list(side), axis=1) if len(terms) > 1 else side[0] for side in zip(*terms)]
        self.got = [up(self.sent[0]), down(self.sent[1])]

    def land(self, got):
        at = 0
        for ring, width in zip(self.rings, self.widths):
            ring.going = [side[:, at : at + width] for side in got]
            at += width


def meet(*arrays):
    return lax.optimization_barrier(arrays)


def per_device(grad_parts, momentum, band):
    z, yh = lax.axis_index("z"), lax.axis_index("yh")
    where = jnp.stack([z, yh]).astype(jnp.int32)
    grad = grad_parts[0, 0]
    mom = momentum[0]

    first = dct_table(band // SPAN)
    second_table = dct_table(band % SPAN)
    second = jnp.tile(second_table, (1, COLS // SPAN))
    block_of = np.arange(COLS) // SPAN
    ones = np.zeros((2, COLS, 128), np.float32)
    for half in range(2):
        ones[half, np.arange(COLS), half * 64 + block_of] = 1.0
    spread = jnp.asarray(ones[0, :, : COLS // SPAN].T, jnp.bfloat16)
    ones = jnp.asarray(ones, jnp.bfloat16)
    same = jnp.asarray(np.kron(np.eye(2), np.ones((SPAN, SPAN))), jnp.bfloat16)

    def owner(k):
        return lax.rem(z + k + NZ, NZ)

    def z_block(at):
        def block(k):
            rows = lax.dynamic_slice(grad, (owner(k) * 2 * SPAN, at), (2 * SPAN, CHUNK))
            return rows.astype(jnp.float32)

        return block

    def y_block(got):
        def block(k):
            rows = lax.dynamic_slice(grad, ((owner(k) * 2 + yh) * SPAN, Y_AT), (SPAN, Y_COLS))
            term = lax.dynamic_index_in_dim(got, owner(k), 0, keepdims=False) + rows.astype(jnp.float32)
            return jnp.concatenate([term[:, : Y_COLS // 2], term[:, Y_COLS // 2 :]], axis=0)

        return block

    def cross_y(total):
        give = lax.dynamic_slice(total, ((1 - yh) * SPAN, 0), (SPAN, CHUNK))
        keep = lax.dynamic_slice(total, (yh * SPAN, 0), (SPAN, CHUNK))
        return keep, give, flip(give, "yh", 2, 1)

    ring_a, ring_b = Ring(z_block(0), CHUNK), Ring(z_block(CHUNK), CHUNK)
    a = Flight(ring_a)
    ring_b.first = meet(ring_b.first, *a.sent)[0]
    b = Flight(ring_b)
    rows = after(grad, *b.sent).reshape(NZ, 2 * SPAN, COLS)
    give = lax.dynamic_slice(rows, (0, (1 - yh) * SPAN, Y_AT), (NZ, SPAN, Y_COLS)).astype(jnp.float32)
    got = flip(give, "yh", 2, 1)

    a.land(meet(*a.got, give)[:2])
    a = Flight(ring_a)

    b.land(meet(*b.got, *a.sent)[:2])
    b = Flight(ring_b)
    coeffs = partial_coeffs(where, grad, after(mom, *b.sent), first, second, ones)
    pair = second[:, :128]
    gram = jnp.dot(first, first.T, precision=HIGHEST) * jnp.dot(second_table, second_table.T, precision=HIGHEST)

    coeffs, pair, *rest = meet(coeffs, pair, *a.got)
    a.land(rest)
    a = Flight(ring_a)

    got, coeffs, *rest = meet(got, coeffs, *b.got, *a.sent)
    b.land(rest[:2])
    ring_y = Ring(y_block(got), Y_COLS // 2)
    b = Flight(ring_b, ring_y)
    for axis, size, bit in (("c", 2, 1), ("x", 4, 1)):
        coeffs = coeffs + flip(coeffs, axis, size, bit)

    coeffs, *rest = meet(coeffs, *a.got, *b.sent)
    a.land(rest[:2])
    a = Flight(ring_a)
    coeffs = coeffs + flip(coeffs, "x", 4, 2)
    side = (z // 2) % 2
    pairs = coeffs.reshape(2, 2, 2, BAND, 128)
    keep = lax.dynamic_index_in_dim(pairs, side, 1, keepdims=False).reshape(4, BAND, 128)
    other = lax.dynamic_index_in_dim(pairs, 1 - side, 1, keepdims=False).reshape(4, BAND, 128)
    more = flip(other, "z", NZ, 2)

    keep, more, *rest = meet(keep, more, *b.got, *a.sent)
    b.land(rest[:2])
    b = Flight(ring_b, ring_y)
    coeffs = after(keep, *b.sent) + more
    coeffs = coeffs + flip(coeffs, "yl", 2, 1)

    coeffs, *rest = meet(coeffs, *a.got)
    a.land(rest)
    total = sum(ring_a.parts())
    keep_a = lax.dynamic_slice(total, (yh * SPAN, 0), (SPAN, CHUNK))
    give_a = lax.dynamic_slice(total, ((1 - yh) * SPAN, 0), (SPAN, CHUNK))
    flat = coeffs.reshape(2, SPAN, 128)
    got_a = flip(jnp.concatenate([give_a, flat[0], flat[1]], axis=1), "yh", 2, 1)
    got_a, more = got_a[:, :CHUNK], got_a[:, CHUNK:]
    coeffs = coeffs + jnp.stack([more[:, :128], more[:, 128:]]).reshape(4, BAND, 128)
    more = flip(coeffs, "z", NZ, 4)
    front = finish(None, mom, 0, CHUNK, [keep_a, after(got_a, coeffs)], first, pair, same)

    coeffs, front, *rest = meet(coeffs, front, *b.got)
    b.land(rest)
    y = Flight(ring_y)
    keep_b, give_b, got_b = cross_y(after(sum(ring_b.parts()), *y.sent))
    coeffs = after(coeffs, give_b) + more
    more = flip(coeffs, "z", NZ, 1)

    coeffs, *rest = meet(coeffs, *y.got)
    y.land(rest)
    y = Flight(ring_y)

    squares, average = average_of(where, after(coeffs, *y.sent), more, gram, first, second, spread)
    more = flip(squares, "z", NZ, 2)
    front = finish(front, mom, CHUNK, CHUNK, [keep_b, after(got_b, average)], first, pair, same)

    front, average, squares, more, *rest = meet(front, average, squares, more, *y.got)
    y.land(rest)
    momentum, step_dir = last(
        front, squares, more, average, mom, Y_AT, Y_COLS, ring_y.parts(), first, pair, same
    )
    return (momentum[None], step_dir)


def solution(mesh):
    fine = Mesh(mesh.devices.reshape(4, 2, 2, NZ, 2), ("x", "yl", "c", "z", "yh"))
    rep, fsdp = ("x", "yl", "c"), ("z", "yh")
    return jax.shard_map(
        per_device,
        mesh=fine,
        in_specs=(P(rep, fsdp, None, None), P(rep, fsdp, None), P()),
        out_specs=(P(rep, fsdp, None), P(fsdp, None)),
        check_vma=False,
    )
```

```python
import functools

import jax
import jax.numpy as jnp
import numpy as np
from jax import lax
from jax.experimental import pallas as pl
from jax.experimental.pallas import tpu as pltpu
from jax.sharding import Mesh, PartitionSpec as P

SPAN = 64
BAND = 32
COLS = 4096
ROWS = 1024
NZ = 8
REPS = 16
HIGHEST = lax.Precision.HIGHEST
VMEM_LIMIT = 16 * 1024 * 1024
NO_COST = pl.CostEstimate(flops=0, bytes_accessed=0, transcendentals=0)

CHUNK, Y_COLS = 1536, 1024
Y_AT = 2 * CHUNK


def dct_table(index):
    pos = jnp.arange(SPAN).astype(jnp.float32)
    freq = index.astype(jnp.float32)[:, None]
    table = jnp.cos(jnp.pi * (2.0 * pos[None, :] + 1.0) * freq / (2.0 * SPAN)) * jnp.sqrt(
        2.0 / SPAN
    )
    return jnp.where(index[:, None] == 0, jnp.sqrt(1.0 / SPAN) * jnp.ones_like(table), table)


def thirds(x):
    high = x.astype(jnp.bfloat16)
    rest = x - high.astype(jnp.float32)
    middle = rest.astype(jnp.bfloat16)
    low = (rest - middle.astype(jnp.float32)).astype(jnp.bfloat16)
    return high, middle, low


def dot(a, b):
    return jnp.dot(a, b, preferred_element_type=jnp.float32)


def add_thirds(stacked):
    n = stacked.shape[0] // 3
    return (stacked[2 * n :] + stacked[n : 2 * n]) + stacked[:n]


def along_blocks(x, ones):
    return add_thirds(dot(jnp.concatenate(thirds(x), axis=0), ones))


def partial_coeffs_kernel(where_ref, grad_ref, mom_ref, first_ref, second_ref, ones_ref, out_ref):
    first3 = jnp.concatenate(thirds(first_ref[...]), axis=0)
    total = jnp.zeros((BAND, 128), jnp.float32)
    for half in range(2):
        rows = grad_ref[half * SPAN : (half + 1) * SPAN, :]
        along = add_thirds(dot(first3, rows)) * second_ref[...]
        total += along_blocks(along, ones_ref[half])
    out_ref[0] = total

    @pl.when(pl.program_id(0) == where_ref[0])
    def _():
        along = jnp.dot(
            first_ref[...], mom_ref[...], precision=HIGHEST, preferred_element_type=jnp.float32
        )
        along = (0.9 * along) * second_ref[...]
        out_ref[0] += along_blocks(along, ones_ref[where_ref[1]])


def partial_coeffs(where, grad, mom, first, second, ones):
    fixed = lambda shape: pl.BlockSpec(shape, lambda i, w: (0,) * len(shape))
    return pl.pallas_call(
        partial_coeffs_kernel,
        out_shape=jax.ShapeDtypeStruct((NZ, BAND, 128), jnp.float32),
        grid_spec=pltpu.PrefetchScalarGridSpec(
            num_scalar_prefetch=1,
            grid=(NZ,),
            in_specs=[
                pl.BlockSpec((2 * SPAN, COLS), lambda i, w: (i, 0)),
                fixed((SPAN, COLS)),
                fixed((BAND, SPAN)),
                fixed((BAND, COLS)),
                fixed((2, COLS, 128)),
            ],
            out_specs=pl.BlockSpec((1, BAND, 128), lambda i, w: (i, 0, 0)),
        ),
        compiler_params=pltpu.CompilerParams(vmem_limit_bytes=2 * VMEM_LIMIT),
        cost_estimate=NO_COST,
        name="partial_coeffs",
    )(where, grad, mom, first, second, ones)


def new_momentum(mom_ref, parts, first_ref, second_ref, same_ref):
    grad = parts[0][...]
    for part in parts[1:]:
        grad = grad + part[...]
    if grad.shape[0] == 2 * SPAN:
        grad = jnp.concatenate([grad[:SPAN], grad[SPAN:]], axis=1)
    mom = 0.9 * mom_ref[...] + grad
    first, second = first_ref[...], second_ref[...]
    along = jnp.dot(first, mom, precision=HIGHEST, preferred_element_type=jnp.float32)
    spread = [
        along_blocks(along[:, c : c + 128] * second, same_ref[...]) * second
        for c in range(0, mom.shape[1], 128)
    ]
    own = lax.dot_general(
        first, jnp.concatenate(spread, axis=1), (((0,), (0,)), ((), ())), precision=HIGHEST,
        preferred_element_type=jnp.float32,
    )
    return mom - own


def finish_kernel(has_front, mom_ref, *refs):
    *parts, first_ref, second_ref, same_ref, out_ref = refs[has_front:]
    out_ref[...] = new_momentum(mom_ref, parts, first_ref, second_ref, same_ref)


def whole(x):
    return pl.BlockSpec(x.shape, lambda i: (0, 0))


def finish(front, mom, at, width, parts, first, second, same):
    front = [] if front is None else [front]
    others = (*parts, first, second, same)
    columns = pl.BlockSpec((SPAN, width), lambda i: (0, at // width))
    return pl.pallas_call(
        functools.partial(finish_kernel, len(front)),
        out_shape=jax.ShapeDtypeStruct((SPAN, COLS), jnp.float32),
        grid=(1,),
        in_specs=[columns, *[pl.BlockSpec(memory_space=pl.ANY)] * len(front), *map(whole, others)],
        out_specs=columns,
        input_output_aliases={1: 0} if front else {},
        compiler_params=pltpu.CompilerParams(vmem_limit_bytes=VMEM_LIMIT),
        cost_estimate=NO_COST,
        name="finish",
    )(mom, *front, *others)


def last_kernel(front_ref, squares_ref, more_ref, average_ref, mom_ref, *refs):
    *parts, first_ref, second_ref, same_ref, out_ref, dir_ref = refs
    mean_square = jnp.sum(squares_ref[...] + more_ref[...]) / (ROWS * COLS) + 1e-06
    scale = lax.rsqrt(mean_square)
    scale = scale * (1.5 - 0.5 * (mean_square * scale) * scale)
    dir_ref[...] = average_ref[...] * scale
    out_ref[...] = new_momentum(mom_ref, parts, first_ref, second_ref, same_ref)


def last(front, squares, more, average, mom, at, width, parts, first, second, same):
    before, others = (squares, more, average), (*parts, first, second, same)
    out = jax.ShapeDtypeStruct((SPAN, COLS), jnp.float32)
    columns = pl.BlockSpec((SPAN, width), lambda i: (0, at // width))
    return pl.pallas_call(
        last_kernel,
        out_shape=[out, out],
        grid=(1,),
        in_specs=[pl.BlockSpec(memory_space=pl.ANY), *map(whole, before), columns, *map(whole, others)],
        out_specs=[columns, whole(out)],
        input_output_aliases={0: 0},
        compiler_params=pltpu.CompilerParams(vmem_limit_bytes=VMEM_LIMIT),
        cost_estimate=NO_COST,
        name="last",
    )(front, *before, mom, *others)


def average_kernel(where_ref, coeffs_ref, more_ref, gram_ref, first_ref, second_ref, spread_ref, squares_ref, out_ref):
    total = jnp.zeros((BAND, 128), jnp.float32)
    for i in range(coeffs_ref.shape[0]):
        coeffs = (coeffs_ref[i] + more_ref[i]) * (1.0 / REPS)
        total += coeffs * jnp.dot(
            gram_ref[...], coeffs, precision=HIGHEST, preferred_element_type=jnp.float32
        )
    squares_ref[...] = (total[:8] + total[8:16]) + (total[16:24] + total[24:])
    row = lax.div(where_ref[0], 4) * 2 + lax.rem(where_ref[0], 2)
    coeffs = (coeffs_ref[row] + more_ref[row]) * (1.0 / REPS)
    half = COLS // SPAN
    coeffs = jnp.where(where_ref[1] == 0, coeffs[:, :half], coeffs[:, half:])
    along = along_blocks(coeffs, spread_ref[...]) * second_ref[...]
    out_ref[...] = lax.dot_general(
        first_ref[...], along, (((0,), (0,)), ((), ())), precision=HIGHEST,
        preferred_element_type=jnp.float32,
    )


def average_of(where, coeffs, more, gram, first, second, spread):
    vmem = pl.BlockSpec(memory_space=pltpu.VMEM)
    return pl.pallas_call(
        average_kernel,
        out_shape=[jax.ShapeDtypeStruct((8, 128), jnp.float32), jax.ShapeDtypeStruct((SPAN, COLS), jnp.float32)],
        in_specs=[pl.BlockSpec(memory_space=pltpu.SMEM)] + [vmem] * 6,
        compiler_params=pltpu.CompilerParams(vmem_limit_bytes=VMEM_LIMIT),
        cost_estimate=NO_COST,
        name="average",
    )(where, coeffs, more, gram, first, second, spread)


def flip(x, axis, size, bit):
    return lax.ppermute(x, axis, [(i, i ^ bit) for i in range(size)])


def up(x):
    return lax.ppermute(x, "z", [(i, (i + 1) % NZ) for i in range(NZ)])


def down(x):
    return lax.ppermute(x, "z", [(i, (i - 1) % NZ) for i in range(NZ)])


def after(x, *earlier):
    return lax.optimization_barrier((x, *earlier))[0]


def add_four(terms):
    own, one, two, three = terms
    return (own + one) + (two + three)


def swap(x, axes, flips):
    sizes = [lax.axis_size(axis) for axis in axes]
    places = list(np.ndindex(*sizes))
    index = lambda place: int(np.ravel_multi_index(place, sizes))
    return lax.ppermute(x, axes, [(index(p), index([i ^ f for i, f in zip(p, flips)])) for p in places])


def swap_three(x, axes, one, two):
    return [x] + [swap(x, axes, flips) for flips in ((one, 0), (0, two), (one, two))]


class Ring:
    def __init__(self, block, width):
        self.block, self.width = block, width
        self.step = 4
        self.first = block(4)
        self.going = None

    def next(self):
        half = self.width // 2
        if self.step == 4:
            terms = self.first[:, :half], self.first[:, half:]
        else:
            upward, downward = self.going
            if self.step == 3:
                zeros = jnp.zeros((upward.shape[0], half), jnp.float32)
                upward = jnp.concatenate([upward, zeros], axis=1)
                downward = jnp.concatenate([zeros, downward], axis=1)
            terms = self.block(self.step) + upward, self.block(-self.step) + downward
        self.step -= 1
        return terms

    def parts(self):
        return [self.block(0), *self.going]


class Flight:
    def __init__(self, *rings):
        self.rings = rings
        terms = [ring.next() for ring in rings]
        self.widths = [up_term.shape[1] for up_term, _ in terms]
        self.sent = [jnp.concatenate(list(side), axis=1) if len(terms) > 1 else side[0] for side in zip(*terms)]
        self.got = [up(self.sent[0]), down(self.sent[1])]

    def land(self, got):
        at = 0
        for ring, width in zip(self.rings, self.widths):
            ring.going = [side[:, at : at + width] for side in got]
            at += width


def meet(*arrays):
    return lax.optimization_barrier(arrays)


def per_device(grad_parts, momentum, band):
    z, yh = lax.axis_index("z"), lax.axis_index("yh")
    where = jnp.stack([z, yh]).astype(jnp.int32)
    grad = grad_parts[0, 0]
    mom = momentum[0]

    first = dct_table(band // SPAN)
    second_table = dct_table(band % SPAN)
    second = jnp.tile(second_table, (1, COLS // SPAN))
    block_of = np.arange(COLS) // SPAN
    ones = np.zeros((2, COLS, 128), np.float32)
    for half in range(2):
        ones[half, np.arange(COLS), half * 64 + block_of] = 1.0
    spread = jnp.asarray(ones[0, :, : COLS // SPAN].T, jnp.bfloat16)
    ones = jnp.asarray(ones, jnp.bfloat16)
    same = jnp.asarray(np.kron(np.eye(2), np.ones((SPAN, SPAN))), jnp.bfloat16)

    def owner(k):
        return lax.rem(z + k + NZ, NZ)

    def z_block(at):
        def block(k):
            rows = lax.dynamic_slice(grad, (owner(k) * 2 * SPAN, at), (2 * SPAN, CHUNK))
            return rows.astype(jnp.float32)

        return block

    def y_rows(rows, k, half):
        return lax.dynamic_slice(rows, ((owner(k) * 2 + half) * SPAN, Y_AT), (SPAN, Y_COLS)).astype(jnp.float32)

    def y_give(rows, places):
        return jnp.concatenate([y_rows(rows, k, 1 - yh) for k in places], axis=0)

    def y_block(got):
        def block(k):
            term = got[k] + y_rows(grad, k, yh)
            return jnp.concatenate([term[:, : Y_COLS // 2], term[:, Y_COLS // 2 :]], axis=0)

        return block

    def by_place(places, rows):
        return {k: rows[i * SPAN : (i + 1) * SPAN] for i, k in enumerate(places)}

    def cross_y(total):
        give = lax.dynamic_slice(total, ((1 - yh) * SPAN, 0), (SPAN, CHUNK))
        keep = lax.dynamic_slice(total, (yh * SPAN, 0), (SPAN, CHUNK))
        return keep, give, flip(give, "yh", 2, 1)

    ring_a, ring_b = Ring(z_block(0), CHUNK), Ring(z_block(CHUNK), CHUNK)
    a = Flight(ring_a)
    ring_b.first = meet(ring_b.first, *a.sent)[0]
    b = Flight(ring_b)
    far, near = (4, 3, -3, 2, -2), (1, -1, 0)
    give = y_give(after(grad, *b.sent), far)
    got_far = flip(give, "yh", 2, 1)

    a.land(meet(*a.got, give)[:2])
    a = Flight(ring_a)

    b.land(meet(*b.got, *a.sent)[:2])
    b = Flight(ring_b)
    coeffs = partial_coeffs(where, grad, after(mom, *b.sent), first, second, ones)
    pair = second[:, :128]
    gram = jnp.dot(first, first.T, precision=HIGHEST) * jnp.dot(second_table, second_table.T, precision=HIGHEST)

    got_far, coeffs, pair, *rest = meet(got_far, coeffs, pair, *a.got)
    a.land(rest)
    got = by_place(far, got_far)
    ring_y = Ring(y_block(got), Y_COLS // 2)
    a = Flight(ring_a, ring_y)
    got_near = flip(y_give(after(grad, *a.sent), near), "yh", 2, 1)

    coeffs, *rest = meet(coeffs, *b.got, *a.sent)
    b.land(rest[:2])
    b = Flight(ring_b)
    coeffs, got_near = meet(coeffs, got_near, *b.sent)[:2]
    got.update(by_place(near, got_near))
    for axis, size, bit in (("c", 2, 1), ("x", 4, 1)):
        coeffs = coeffs + flip(coeffs, axis, size, bit)

    coeffs, *rest = meet(coeffs, *a.got, *b.sent)
    side = (z // 2) % 2
    pairs = coeffs.reshape(2, 2, 2, BAND, 128)
    keep = lax.dynamic_index_in_dim(pairs, side, 1, keepdims=False).reshape(4, BAND, 128)
    other = lax.dynamic_index_in_dim(pairs, 1 - side, 1, keepdims=False).reshape(4, BAND, 128)
    more = flip(other, "z", NZ, 2)
    a.land(meet(*rest[:2], other)[:2])
    a = Flight(ring_a, ring_y)

    keep, more, *rest = meet(keep, more, *b.got, *a.sent)
    b.land(rest[:2])
    b = Flight(ring_b)
    coeffs = after(keep, *b.sent) + more
    for axis, size, bit in (("x", 4, 2), ("yl", 2, 1)):
        coeffs = coeffs + flip(coeffs, axis, size, bit)

    coeffs, *rest = meet(coeffs, *a.got)
    a.land(rest)
    total = sum(ring_a.parts())
    keep_a = lax.dynamic_slice(total, (yh * SPAN, 0), (SPAN, CHUNK))
    give_a = lax.dynamic_slice(total, ((1 - yh) * SPAN, 0), (SPAN, CHUNK))
    flat = coeffs.reshape(2, SPAN, 128)
    got_a = flip(jnp.concatenate([give_a, flat[0], flat[1]], axis=1), "yh", 2, 1)
    y = Flight(ring_y)
    got_a, more = got_a[:, :CHUNK], got_a[:, CHUNK:]
    coeffs = coeffs + jnp.stack([more[:, :128], more[:, 128:]]).reshape(4, BAND, 128)
    more = flip(coeffs, "z", NZ, 4)
    front = finish(None, mom, 0, CHUNK, [keep_a, after(got_a, coeffs)], first, pair, same)

    coeffs, front, *rest = meet(coeffs, front, *b.got)
    b.land(rest)
    keep_b, give_b, got_b = cross_y(sum(ring_b.parts()))
    coeffs = after(coeffs, give_b) + more
    more = flip(coeffs, "z", NZ, 1)

    coeffs, *rest = meet(coeffs, *y.got)
    y.land(rest)
    y = Flight(ring_y)

    squares, average = average_of(where, after(coeffs, *y.sent), more, gram, first, second, spread)
    more = flip(squares, "z", NZ, 2)
    front = finish(front, mom, CHUNK, CHUNK, [keep_b, after(got_b, average)], first, pair, same)

    front, average, squares, more, *rest = meet(front, average, squares, more, *y.got)
    y.land(rest)
    momentum, step_dir = last(
        front, squares, more, average, mom, Y_AT, Y_COLS, ring_y.parts(), first, pair, same
    )
    return (momentum[None], step_dir)


def solution(mesh):
    fine = Mesh(mesh.devices.reshape(4, 2, 2, NZ, 2), ("x", "yl", "c", "z", "yh"))
    rep, fsdp = ("x", "yl", "c"), ("z", "yh")
    return jax.shard_map(
        per_device,
        mesh=fine,
        in_specs=(P(rep, fsdp, None, None), P(rep, fsdp, None), P()),
        out_specs=(P(rep, fsdp, None), P(fsdp, None)),
        check_vma=False,
    )
```
